256 devices in a mesh: group: 8 (over x, core), leaf: 32 (over z, y).
Axes of the slice: x: 4, y: 4, z: 8, core: 2. Of those that a mesh axis runs over, the one named last changes fastest.
Arguments:
- panel_values: bfloat16 [64, 1048576], P(None, ('group', 'leaf')), may hold values from -6 to 6
- cluster_basis: bfloat16 [64, 1048576], P(None, ('group', 'leaf')), may hold values from -0.375 to 0.375
- near_blocks: bfloat16 [4096, 3, 256, 256], P(('group', 'leaf')), may hold values from -0.21875 to 0.21875
- near_list: int32 [4096, 3], P(('group', 'leaf')), may hold values from 0 to 4095, as said below
- transfer_leaf: bfloat16 [64, 262144], P(None, ('group', 'leaf')), may hold values from -0.375 to 0.375
- transfer_device: bfloat16 [64, 16384], replicated, may hold values from -0.5 to 0.5
- leaf_coupling: bfloat16 [64, 1572864], P(None, ('group', 'leaf')), may hold values from -0.3125 to 0.3125
- leaf_list: int32 [4096, 6], P(('group', 'leaf')), may hold values from 0 to 4095, as said below
- device_coupling: bfloat16 [64, 65536], P(None, ('group', 'leaf')), may hold values from -0.1875 to 0.1875
- device_list: int32 [256, 4], P(('group', 'leaf')), may hold values from 0 to 255, as said below
- group_coupling: bfloat16 [64, 1024], P(None, 'group'), may hold values from -0.125 to 0.125
- group_list: int32 [8, 2], P('group'), may hold values from 0 to 7, as said below
Outputs:
- product: bfloat16 [64, 1048576], P(None, ('group', 'leaf'))
The draws below stay inside these ranges and needn't reach their ends.
Inputs may be any that keep to these rules, and one draw needn't show every extreme that they name: `near_list`: row t holds t itself first, then 3 - 1 distinct other leaves of the same group cluster, each at most 8 away from t. `leaf_list`: each row holds distinct leaves of the same group cluster as its leaf t, each more than 8 and at most 16 away from t. `device_list`: each row holds distinct device clusters of the same group cluster as its device cluster d, each 2 or more away from d. `group_list`: each row holds distinct group clusters other than its own.
All inputs are finite; a program needn't handle non-finite values.
Results may differ from the reference program's by a relative error of at most 0.0095.
Values may be sent and summed in bfloat16 or wider, within the bound.
A program may use at most 64 MiB of HBM per device.

```python
import jax
import jax.numpy as jnp
from jax import lax

LS = 256
K = 64
R = 64
LPD = 16
NN = 3
NR = 8
C0 = 6
C1 = 4
C2 = 2
GROUPS = 8
SPAN = 32
DEVS = 256
NLEAF = 4096
PANELS = 1048576


def both_sides(nearest, farthest):
    steps_out = jnp.arange(nearest, farthest + 1, dtype=jnp.int32)
    return jnp.concatenate([-steps_out, steps_out]).astype(jnp.int32)


def choose_sources(key, anchor, low_edge, high_edge, offsets, count):
    row_count = anchor.shape[0]
    cand_count = offsets.shape[0]
    scores = jax.random.randint(key, (row_count, cand_count), 0, 1 << 20, dtype=jnp.int32) * cand_count + jnp.arange(cand_count, dtype=jnp.int32)[None, :]
    target = anchor[:, None] + offsets[None, :]
    usable = (target >= low_edge[:, None]) & (target < high_edge[:, None])
    scores = jnp.where(usable, scores, scores + (1 << 28))
    ranking = jnp.argsort(scores, axis=1, stable=True)[:, :count]
    return jnp.take_along_axis(target, ranking, axis=1).astype(jnp.int32)


def draw_near_list(key, part):
    key = jax.random.fold_in(key, 11)
    anchor = jnp.arange(NLEAF, dtype=jnp.int32)
    group_leaves = LPD * SPAN
    low_edge = anchor // group_leaves * group_leaves
    others = choose_sources(key, anchor, low_edge, low_edge + group_leaves, both_sides(1, NR), NN - 1)
    return jnp.concatenate([anchor[:, None], others], axis=1).astype(jnp.int32)


def draw_leaf_list(key, part):
    key = jax.random.fold_in(key, 23)
    anchor = jnp.arange(NLEAF, dtype=jnp.int32)
    group_leaves = LPD * SPAN
    low_edge = anchor // group_leaves * group_leaves
    return choose_sources(key, anchor, low_edge, low_edge + group_leaves, both_sides(NR + 1, LPD), C0)


def draw_device_list(key, part):
    key = jax.random.fold_in(key, 37)
    anchor = jnp.arange(DEVS, dtype=jnp.int32)
    low_edge = anchor // SPAN * SPAN
    return choose_sources(key, anchor, low_edge, low_edge + SPAN, both_sides(2, SPAN - 1), C1)


def draw_group_list(key, part):
    key = jax.random.fold_in(key, 41)
    anchor = jnp.arange(GROUPS, dtype=jnp.int32)
    low_edge = jnp.zeros((GROUPS,), jnp.int32)
    return choose_sources(key, anchor, low_edge, low_edge + GROUPS, both_sides(1, GROUPS - 1), C2)


def level_of(key, shape, shards, low, largest):
    gain = 1.0
    for dim, shards_of in shards:
        draws = jax.random.uniform(jax.random.fold_in(jax.random.fold_in(key, 6), dim), (shards_of,), jnp.float32, low / len(shards), largest / len(shards))
        gain = gain * jnp.repeat(jnp.exp(draws), shape[dim] // shards_of).reshape((-1,) + (1,) * (len(shape) - 1 - dim))
    return gain


def gaussian(own_key, dims, spread, bound, split=(), kind=jnp.bfloat16):
    entries = jax.random.normal(own_key, dims, jnp.float32) * spread
    if len(split) > 0:
        entries = level_of(own_key, dims, split, -0.22, 0.18) * entries
    return jnp.clip(entries, min=-bound, max=bound).astype(kind)


def setup_inputs(seed: int = 0) -> dict:
    splits = jax.random.split(jax.random.key(seed), 13)
    panel_values = gaussian(splits[0], (R, PANELS), 1.0, 6.0, ((1, 256),))
    cluster_basis = gaussian(splits[1], (K, PANELS), LS ** -0.5, 0.375, ((1, 256),))
    near_blocks = gaussian(splits[2], (NLEAF, NN, LS, LS), (NN * LS) ** -0.5, 0.21875, ((0, 256),))
    near_list = draw_near_list(jax.random.fold_in(splits[12], 71), 0)
    transfer_leaf = gaussian(splits[4], (K, NLEAF * K), (LPD * K // 4) ** -0.5, 0.375, ((1, 256),))
    transfer_device = gaussian(splits[5], (K, DEVS * K), (SPAN * K // 16) ** -0.5, 0.5)
    leaf_coupling = gaussian(splits[6], (K, NLEAF * C0 * K), (C0 * K) ** -0.5, 0.3125, ((1, 256),))
    leaf_list = draw_leaf_list(jax.random.fold_in(splits[12], 71), 0)
    device_coupling = gaussian(splits[8], (K, DEVS * C1 * K), (C1 * K * 4) ** -0.5, 0.1875, ((1, 256),))
    device_list = draw_device_list(jax.random.fold_in(splits[12], 71), 0)
    group_coupling = gaussian(splits[10], (K, GROUPS * C2 * K), (C2 * K * 16) ** -0.5, 0.125, ((1, 8),))
    group_list = draw_group_list(jax.random.fold_in(splits[12], 71), 0)
    return {"panel_values": panel_values, "cluster_basis": cluster_basis, "near_blocks": near_blocks, "near_list": near_list, "transfer_leaf": transfer_leaf, "transfer_device": transfer_device, "leaf_coupling": leaf_coupling, "leaf_list": leaf_list, "device_coupling": device_coupling, "device_list": device_list, "group_coupling": group_coupling, "group_list": group_list}


def reference(panel_values, cluster_basis, near_blocks, near_list, transfer_leaf, transfer_device, leaf_coupling, leaf_list, device_coupling, device_list, group_coupling, group_list):
    panel_rows = panel_values.reshape(R, NLEAF, LS)
    basis_rows = cluster_basis.reshape(K, NLEAF, LS).astype(jnp.float32)
    leaf_coefs = jnp.einsum("rtp,ktp->rtk", panel_rows.astype(jnp.float32), basis_rows).astype(jnp.bfloat16)
    up_blocks = transfer_leaf.reshape(K, DEVS, LPD, K).astype(jnp.float32)
    device_coefs = jnp.einsum("rdlb,adlb->rda", leaf_coefs.reshape(R, DEVS, LPD, K).astype(jnp.float32), up_blocks).astype(jnp.bfloat16)
    top_blocks = transfer_device.reshape(K, GROUPS, SPAN, K).astype(jnp.float32)
    group_coefs = jnp.einsum("rgsb,agsb->rga", device_coefs.reshape(R, GROUPS, SPAN, K).astype(jnp.float32), top_blocks).astype(jnp.bfloat16)
    group_sources = group_coefs[:, group_list].astype(jnp.float32)
    group_local = jnp.einsum("rgjc,bgjc->rgb", group_sources, group_coupling.reshape(K, GROUPS, C2, K).astype(jnp.float32)).astype(jnp.bfloat16)
    device_sources = device_coefs[:, device_list].astype(jnp.float32)
    device_local = jnp.einsum("rdjc,bdjc->rdb", device_sources, device_coupling.reshape(K, DEVS, C1, K).astype(jnp.float32))
    device_local = device_local + jnp.einsum("rga,agsb->rgsb", group_local.astype(jnp.float32), top_blocks).reshape(R, DEVS, K)
    device_local = device_local.astype(jnp.bfloat16)
    leaf_sources = leaf_coefs[:, leaf_list].astype(jnp.float32)
    leaf_local = jnp.einsum("rtjc,btjc->rtb", leaf_sources, leaf_coupling.reshape(K, NLEAF, C0, K).astype(jnp.float32))
    leaf_local = leaf_local + jnp.einsum("rda,adlb->rdlb", device_local.astype(jnp.float32), up_blocks).reshape(R, NLEAF, K)
    leaf_local = leaf_local.astype(jnp.bfloat16)
    far_part = jnp.einsum("rtk,ktp->rtp", leaf_local.astype(jnp.float32), basis_rows)

    def near_piece(pieces):
        blocks, lists = pieces
        sources = jnp.take(panel_rows, lists, axis=1).astype(jnp.float32)
        return jnp.einsum("rtjq,tjpq->rtp", sources, blocks.astype(jnp.float32))

    near_part = lax.map(near_piece, (near_blocks.reshape(DEVS, LPD, NN, LS, LS), near_list.reshape(DEVS, LPD, NN)))
    near_part = jnp.transpose(near_part, (1, 0, 2, 3)).reshape(R, NLEAF, LS)
    return (far_part + near_part).astype(jnp.bfloat16).reshape(R, PANELS)
```

```python
import functools

import jax
import jax.numpy as jnp
from jax import lax
from jax.experimental import pallas as pl
from jax.experimental.pallas import tpu as pltpu
from jax.sharding import PartitionSpec as P

ROW = 4
MESH = pl.DeviceIdType.MESH
F32 = jnp.float32
BF16 = jnp.bfloat16


def nt(a, b):
    return lax.dot_general(a, b, (((1,), (1,)), ((), ())), preferred_element_type=F32)


def nn(a, b):
    return jnp.dot(a, b, preferred_element_type=F32)


def low_lanes(shape):
    return lax.broadcasted_iota(jnp.int32, shape, 1) % 128 < 64


def fold_rows(wide):
    half = wide.shape[0] // 2
    return jnp.where(low_lanes((half, 128)), wide[:half], wide[half:])


def unfold_rows(packed):
    low = low_lanes(packed.shape)
    zero = jnp.zeros_like(packed)
    return jnp.concatenate([jnp.where(low, packed, zero), jnp.where(low, zero, packed)], axis=0)


def spreader():
    row = lax.broadcasted_iota(jnp.int32, (128, 256), 0)
    col = lax.broadcasted_iota(jnp.int32, (128, 256), 1)
    return jnp.where(row == col // 128 * 64 + col % 64, 1.0, 0.0).astype(BF16)


def spread(x):
    pieces = [x[:, i : i + 128] for i in range(0, x.shape[1], 128)]
    wide = [nn(piece, spreader()).astype(BF16) for piece in pieces]
    return jnp.concatenate(wide, axis=1)


def clamp(index, count):
    return jnp.minimum(jnp.maximum(index, 0), count - 1)


def kernel(
    groups, span, leaves, rank, ls, leaf_links, device_links, group_links, reach,
    panel, basis, near, near_list, transfer_leaf, transfer_device, leaf_coupling, leaf_list,
    device_coupling, device_list, group_coupling, group_list,
    out,
    p_own, b_own, nb_self, nb_rest, t_own, td_group, lc, dc, gc,
    halo_a, halo_b, c_own, halo_c, dbuf, pgbuf, gbuf,
    w, acc, lf, td_dup,
    load_sem, halo_send, halo_recv, row_send, row_recv, col_send, col_recv, drow_send, drow_recv,
    grp_send, grp_recv,
):
    gi = lax.axis_index("group")
    li = lax.axis_index("leaf")
    zi = li // ROW
    yi = li % ROW
    cols = span // ROW
    first_leaf = (gi * span + li) * leaves
    half = reach // 2
    left = zi * ROW + lax.rem(yi + ROW - 1, ROW)
    right = zi * ROW + lax.rem(yi + 1, ROW)
    at_start, at_end = yi == 0, yi == ROW - 1
    next_z = jnp.where(at_start, lax.rem(zi + 1, cols), lax.rem(zi + cols - 1, cols)) * ROW + yi

    row_peers = [zi * ROW + lax.rem(yi + k, ROW) for k in range(1, ROW)]
    col_peers = [lax.rem(zi + k, cols) * ROW + yi for k in range(1, cols)]
    grp_peers = [lax.rem(gi + k, groups) for k in range(1, groups)]

    barrier = pltpu.get_barrier_semaphore()
    for peer in row_peers + col_peers:
        pl.semaphore_signal(barrier, inc=1, device_id=(gi, peer), device_id_type=MESH)
    for peer in grp_peers:
        pl.semaphore_signal(barrier, inc=1, device_id=(peer, li), device_id_type=MESH)

    def load(i, src, dst):
        copy = pltpu.make_async_copy(src, dst, load_sem.at[i])
        copy.start()
        return copy

    for leaf in range(leaves):
        pltpu.make_async_copy(panel.at[:, pl.ds(leaf * ls, ls)], p_own.at[leaf], load_sem.at[0]).start()
    load_p = pltpu.make_async_copy(p_own, p_own, load_sem.at[0])
    load_b = load(1, basis, b_own)
    load_t = load(2, transfer_leaf, t_own)
    group_start = pl.multiple_of(gi * span * rank, span * rank)
    load_td = load(3, transfer_device.at[:, pl.ds(group_start, span * rank)], td_group)
    load_self = load(4, near.at[:, 0], nb_self)
    load_lc = load(5, leaf_coupling, lc)
    load_gc = load(6, group_coupling, gc)
    load_dc = load(7, device_coupling, dc)
    load_rest = load(8, near.at[:, pl.ds(1, 2)], nb_rest)

    def send(src, dst, send_sem, recv_sem, device):
        copy = pltpu.make_async_remote_copy(
            src_ref=src, dst_ref=dst, send_sem=send_sem, recv_sem=recv_sem,
            device_id=device, device_id_type=MESH,
        )
        copy.start()
        return copy

    low = low_lanes((64, 128))
    load_p.wait()
    load_b.wait()
    for pair in range(leaves // 2):
        wide = []
        for leaf in (2 * pair, 2 * pair + 1):
            basis_leaf = b_own[:, leaf * ls : (leaf + 1) * ls]
            twice = jnp.concatenate([basis_leaf, basis_leaf], axis=0)
            coefs = nt(p_own[leaf], twice)
            w[leaves + leaf] = coefs.astype(BF16)
            wide.append(coefs)
        c_own[:, pair * 128 : (pair + 1) * 128] = jnp.where(low, wide[0], wide[1]).astype(BF16)

    load_t.wait()
    transfer = t_own[...]
    own_d = nt(c_own[...], jnp.concatenate([transfer, transfer], axis=0))
    own_slot = yi * cols + zi
    dbuf[own_slot] = fold_rows(own_d).astype(BF16)

    pl.semaphore_wait(barrier, (ROW - 1) + (cols - 1) + (groups - 1))

    col_copies = [
        send(dbuf.at[own_slot], dbuf.at[own_slot], col_send.at[k], col_recv.at[k], (gi, peer))
        for k, peer in enumerate(col_peers)
    ]
    to_right, to_left = jnp.where(at_end, 2, 0), jnp.where(at_start, 2, 1)
    edges = {
        "c": (halo_c, 0, c_own, c_own),
        "a": (halo_a, 3, p_own.at[pl.ds(leaves - half, half)], p_own.at[pl.ds(0, half)]),
        "b": (halo_b, 6, p_own.at[pl.ds(leaves - 2 * half, half)], p_own.at[pl.ds(half, half)]),
    }
    halo_copies = []

    def halo_copy(name, src, slot, k, device):
        buffer, base = edges[name][:2]
        return pltpu.make_async_remote_copy(
            src_ref=src, dst_ref=buffer.at[slot], send_sem=halo_send.at[base + k],
            recv_sem=halo_recv.at[base + slot], device_id=(gi, device), device_id_type=MESH,
        )

    def send_halo(name):
        for k, (slot, device) in enumerate(((to_right, right), (to_left, left))):
            copy = halo_copy(name, edges[name][2 + k], slot, k, device)
            copy.start()
            halo_copies.append(copy)

    def hand_on(name):
        @pl.when(at_start | at_end)
        def _():
            buffer = edges[name][0]
            halo_copy(name, buffer.at[2], 2, 2, next_z).wait_recv()
            halo_copy(name, buffer.at[2], jnp.where(at_start, 0, 1), 2, next_z).start()

    def wait_halo(name):
        for slot in (0, 1):
            halo_copy(name, edges[name][0].at[2], slot, 2, next_z).wait_recv()

    def end_halo(name):
        @pl.when(at_start | at_end)
        def _():
            halo_copy(name, edges[name][0].at[2], 0, 2, next_z).wait_send()

    send_halo("c")
    send_halo("a")

    load_td.wait()
    for j in range(cols):
        tile = pl.multiple_of((j * ROW + yi - yi % 2) * rank, 128)
        td_dup[:, j * 256 : (j + 1) * 256] = spread(td_group[:, pl.ds(tile, 128)])

    def td_of(j):
        return td_dup[:, pl.ds(pl.multiple_of(j * 256 + yi % 2 * 128, 128), 128)]

    def near_self(first, last):
        for leaf in range(first, last):
            lanes = slice(leaf * ls, (leaf + 1) * ls)
            acc[:, lanes] = nt(p_own[leaf], nb_self[leaf])

    load_self.wait()
    near_self(0, leaves)
    load_gc.wait()
    gc_dup = spread(gc[...])
    load_dc.wait()
    dc_dup = spread(dc[...])
    td_wide = jnp.concatenate([td_of(j) for j in range(cols)], axis=1)
    td_wide = jnp.concatenate([td_wide, td_wide], axis=0)

    for copy in col_copies:
        copy.wait()
    col_d = jnp.concatenate([dbuf[yi * cols + j] for j in range(cols)], axis=1)
    pgbuf[yi] = fold_rows(nt(unfold_rows(col_d), td_wide))
    pg_copies = [
        send(pgbuf.at[yi], pgbuf.at[yi], row_send.at[k], row_recv.at[k], (gi, peer))
        for k, peer in enumerate(row_peers)
    ]
    send_halo("b")
    mine = pl.ds(yi * cols, cols)
    d_copies = [
        send(dbuf.at[mine], dbuf.at[mine], drow_send.at[k], drow_recv.at[k], (gi, peer))
        for k, peer in enumerate(row_peers)
    ]

    hand_on("c")
    hand_on("a")

    for copy in pg_copies:
        copy.wait()
    total = pgbuf[0]
    for j in range(1, ROW):
        total = total + pgbuf[j]
    gbuf[gi] = total.astype(BF16)
    g_copies = [
        send(gbuf.at[gi], gbuf.at[gi], grp_send.at[k], grp_recv.at[k], (peer, li))
        for k, peer in enumerate(grp_peers)
    ]

    hand_on("b")

    load_lc.wait()
    wait_halo("c")
    for slot, start in ((0, 0), (1, 2 * leaves)):
        for pair in range(leaves // 2):
            wide = nn(halo_c[slot, :, pair * 128 : (pair + 1) * 128], spreader()).astype(BF16)
            w[start + 2 * pair] = wide[:, :128]
            w[start + 2 * pair + 1] = wide[:, 128:]

    for pair in range(leaves // 2):
        sources = []
        matrices = []
        for leaf in (2 * pair, 2 * pair + 1):
            found = [w[clamp(leaf_list[j, leaf] - first_leaf + leaves, 3 * leaves)] for j in range(leaf_links)]
            halves = [jnp.where(low, found[j], found[j + 1]) for j in range(0, leaf_links, 2)]
            sources.append(jnp.concatenate(halves, axis=1))
            matrices.append(lc[:, leaf * leaf_links * rank : (leaf + 1) * leaf_links * rank])
        far = nt(jnp.concatenate(sources, axis=0), jnp.concatenate(matrices, axis=0))
        lf[:, pair * 128 : (pair + 1) * 128] = jnp.where(low, far[:64], far[64:])

    def leaf_of(buffer, index, count):
        return buffer[clamp(index, count)]

    def near_source(leaf, source):
        own = leaf_of(p_own, source, leaves)
        if leaf < reach:
            found = jnp.where(source >= 0, own, leaf_of(halo_a.at[0], source + half, half))
            if leaf < half:
                found = jnp.where(source < -half, leaf_of(halo_b.at[0], source + 2 * half, half), found)
        else:
            past = source - leaves
            found = jnp.where(past < 0, own, leaf_of(halo_a.at[1], past, half))
            if leaf >= leaves - half:
                found = jnp.where(past >= half, leaf_of(halo_b.at[1], past - half, half), found)
        return found

    def near_rest(leaf):
        found = [near_source(leaf, near_list[j, leaf] - first_leaf) for j in (1, 2)]
        blocks = [nb_rest[leaf, 0], nb_rest[leaf, 1]]
        return nt(jnp.concatenate(found, axis=1), jnp.concatenate(blocks, axis=1))

    load_rest.wait()
    wait_halo("a")
    for leaf in range(half, leaves - half):
        acc[:, leaf * ls : (leaf + 1) * ls] += near_rest(leaf)

    for copy in d_copies:
        copy.wait()
    places = [clamp(device_list[0, j] - gi * span, span) for j in range(device_links)]
    found = [dbuf[place % ROW * cols + place // ROW] for place in places]
    d_far = nt(unfold_rows(jnp.concatenate(found, axis=1)), dc_dup)
    for copy in g_copies:
        copy.wait()
    found = [gbuf[clamp(group_list[0, j], groups)] for j in range(group_links)]
    g_local = nt(unfold_rows(jnp.concatenate(found, axis=1)), gc_dup).astype(BF16)
    td_own = td_of(zi)[:, :rank]
    d_local = (d_far + nn(g_local, td_own)).astype(BF16)
    l_local = (lf[...] + nn(d_local, t_own[...])).astype(BF16)
    for pair in range(leaves // 2):
        x = l_local[:, pair * 128 : (pair + 1) * 128]
        zero = jnp.zeros_like(x)
        stacked = jnp.concatenate([jnp.where(low, x, zero), jnp.where(low, zero, x)], axis=0)
        first = slice(2 * pair * ls, (2 * pair + 1) * ls)
        second = slice((2 * pair + 1) * ls, (2 * pair + 2) * ls)
        far = nn(stacked, jnp.concatenate([b_own[:, first], b_own[:, second]], axis=0))
        for leaf, lanes, part in ((2 * pair, first, far[:64]), (2 * pair + 1, second, far[64:])):
            if half <= leaf < leaves - half:
                out[:, lanes] = (acc[:, lanes] + part).astype(BF16)
            else:
                acc[:, lanes] = acc[:, lanes] + part

    wait_halo("b")
    for leaf in list(range(half)) + list(range(leaves - half, leaves)):
        lanes = slice(leaf * ls, (leaf + 1) * ls)
        out[:, lanes] = (acc[:, lanes] + near_rest(leaf)).astype(BF16)

    for copy in halo_copies:
        copy.wait_send()
    for name in edges:
        end_halo(name)


def local(
    panel_values,
    cluster_basis,
    near_blocks,
    near_list,
    transfer_leaf,
    transfer_device,
    leaf_coupling,
    leaf_list,
    device_coupling,
    device_list,
    group_coupling,
    group_list,
):
    rhs, width = panel_values.shape
    leaves, near_links, ls, _ = near_blocks.shape
    rank = cluster_basis.shape[0]
    groups = lax.axis_size("group")
    span = lax.axis_size("leaf")
    cols = span // ROW
    reach = leaves // 2
    half = reach // 2
    leaf_links = leaf_list.shape[1]
    device_links = device_list.shape[1]
    group_links = group_list.shape[1]
    coefs = leaves * rank
    hbm = pl.BlockSpec(memory_space=pltpu.HBM)
    smem = pl.BlockSpec(memory_space=pltpu.SMEM)
    sizes = (groups, span, leaves, rank, ls, leaf_links, device_links, group_links, reach)
    dma = pltpu.SemaphoreType.DMA
    halo = pltpu.VMEM((3, half, rhs, ls), BF16)
    return pl.pallas_call(
        functools.partial(kernel, *sizes),
        out_shape=jax.ShapeDtypeStruct((rhs, width), BF16),
        in_specs=[hbm, hbm, hbm, smem, hbm, hbm, hbm, smem, hbm, smem, hbm, smem],
        out_specs=pl.BlockSpec(memory_space=pltpu.VMEM),
        scratch_shapes=[
            pltpu.VMEM((leaves, rhs, ls), BF16),
            pltpu.VMEM((rank, width), BF16),
            pltpu.VMEM((leaves, ls, ls), BF16),
            pltpu.VMEM((leaves, near_links - 1, ls, ls), BF16),
            pltpu.VMEM((rank, coefs), BF16),
            pltpu.VMEM((rank, span * rank), BF16),
            pltpu.VMEM((rank, leaf_links * coefs), BF16),
            pltpu.VMEM((rank, device_links * rank), BF16),
            pltpu.VMEM((rank, group_links * rank), BF16),
            halo,
            halo,
            pltpu.VMEM((rhs, coefs), BF16),
            pltpu.VMEM((3, rhs, coefs), BF16),
            pltpu.VMEM((span, rhs // 2, 2 * rank), BF16),
            pltpu.VMEM((ROW, rhs // 2, 2 * rank), F32),
            pltpu.VMEM((groups, rhs // 2, 2 * rank), BF16),
            pltpu.VMEM((3 * leaves, rhs, 2 * rank), BF16),
            pltpu.VMEM((rhs, width), F32),
            pltpu.VMEM((rhs, coefs), F32),
            pltpu.VMEM((rank, cols * 4 * rank), BF16),
            dma((9,)),
            dma((9,)),
            dma((9,)),
            dma((ROW - 1,)),
            dma((ROW - 1,)),
            dma((cols - 1,)),
            dma((cols - 1,)),
            dma((ROW - 1,)),
            dma((ROW - 1,)),
            dma((groups - 1,)),
            dma((groups - 1,)),
        ],
        compiler_params=pltpu.CompilerParams(
            collective_id=0, has_side_effects=True, vmem_limit_bytes=60 * 1024 * 1024
        ),
        cost_estimate=pl.CostEstimate(flops=500_000_000, bytes_accessed=10_000_000, transcendentals=0),
    )(
        panel_values,
        cluster_basis,
        near_blocks,
        near_list.T,
        transfer_leaf,
        transfer_device,
        leaf_coupling,
        leaf_list.T,
        device_coupling,
        device_list,
        group_coupling,
        group_list,
    )


def solution(mesh):
    in_specs = (
        P(None, ("group", "leaf")),
        P(None, ("group", "leaf")),
        P(("group", "leaf"), None, None, None),
        P(("group", "leaf"), None),
        P(None, ("group", "leaf")),
        P(),
        P(None, ("group", "leaf")),
        P(("group", "leaf"), None),
        P(None, ("group", "leaf")),
        P(("group", "leaf"), None),
        P(None, "group"),
        P("group", None),
    )
    out_specs = P(None, ("group", "leaf"))
    return jax.shard_map(local, mesh=mesh, in_specs=in_specs, out_specs=out_specs, check_vma=False)
```

```python
import functools

import jax
import jax.numpy as jnp
from jax import lax
from jax.experimental import pallas as pl
from jax.experimental.pallas import tpu as pltpu
from jax.sharding import PartitionSpec as P

ROW = 4
MESH = pl.DeviceIdType.MESH
F32 = jnp.float32
BF16 = jnp.bfloat16


def nt(a, b):
    return lax.dot_general(a, b, (((1,), (1,)), ((), ())), preferred_element_type=F32)


def nn(a, b):
    return jnp.dot(a, b, preferred_element_type=F32)


def low_lanes(shape):
    return lax.broadcasted_iota(jnp.int32, shape, 1) % 128 < 64


def fold_rows(wide):
    half = wide.shape[0] // 2
    return jnp.where(low_lanes((half, 128)), wide[:half], wide[half:])


def unfold_rows(packed):
    low = low_lanes(packed.shape)
    zero = jnp.zeros_like(packed)
    return jnp.concatenate([jnp.where(low, packed, zero), jnp.where(low, zero, packed)], axis=0)


def spreader():
    row = lax.broadcasted_iota(jnp.int32, (128, 256), 0)
    col = lax.broadcasted_iota(jnp.int32, (128, 256), 1)
    return jnp.where(row == col // 128 * 64 + col % 64, 1.0, 0.0).astype(BF16)


def spread(x):
    pieces = [x[:, i : i + 128] for i in range(0, x.shape[1], 128)]
    wide = [nn(piece, spreader()).astype(BF16) for piece in pieces]
    return jnp.concatenate(wide, axis=1)


def farthest_first(count):
    return sorted(range(1, count), key=lambda k: -min(k, count - k))


def clamp(index, count):
    return jnp.minimum(jnp.maximum(index, 0), count - 1)


def kernel(
    groups, span, leaves, rank, ls, leaf_links, device_links, group_links, reach,
    panel, basis, near, near_list, transfer_leaf, transfer_device, leaf_coupling, leaf_list,
    device_coupling, device_list, group_coupling, group_list,
    out,
    p_own, b_own, nb_self, nb_rest, t_own, td_group, lc, dc, gc,
    halo_a, halo_b, c_own, halo_c, dbuf, pgbuf, gbuf,
    w, acc, lf, td_dup,
    load_sem, halo_send, halo_recv, row_send, row_recv, col_send, col_recv, drow_send, drow_recv,
    grp_send, grp_recv,
):
    gi = lax.axis_index("group")
    li = lax.axis_index("leaf")
    zi = li // ROW
    yi = li % ROW
    cols = span // ROW
    first_leaf = (gi * span + li) * leaves
    half = reach // 2
    left = zi * ROW + lax.rem(yi + ROW - 1, ROW)
    right = zi * ROW + lax.rem(yi + 1, ROW)
    at_start, at_end = yi == 0, yi == ROW - 1
    next_z = jnp.where(at_start, lax.rem(zi + 1, cols), lax.rem(zi + cols - 1, cols)) * ROW + yi

    row_peers = [zi * ROW + lax.rem(yi + k, ROW) for k in farthest_first(ROW)]
    col_peers = [lax.rem(zi + k, cols) * ROW + yi for k in farthest_first(cols)]
    grp_peers = [lax.rem(gi + k, groups) for k in farthest_first(groups)]

    barrier = pltpu.get_barrier_semaphore()
    for peer in row_peers + col_peers:
        pl.semaphore_signal(barrier, inc=1, device_id=(gi, peer), device_id_type=MESH)
    for peer in grp_peers:
        pl.semaphore_signal(barrier, inc=1, device_id=(peer, li), device_id_type=MESH)

    def load(i, src, dst):
        copy = pltpu.make_async_copy(src, dst, load_sem.at[i])
        copy.start()
        return copy

    for leaf in range(leaves):
        pltpu.make_async_copy(panel.at[:, pl.ds(leaf * ls, ls)], p_own.at[leaf], load_sem.at[0]).start()
    load_p = pltpu.make_async_copy(p_own, p_own, load_sem.at[0])
    load_b = load(1, basis, b_own)
    load_t = load(2, transfer_leaf, t_own)
    group_start = pl.multiple_of(gi * span * rank, span * rank)
    load_td = load(3, transfer_device.at[:, pl.ds(group_start, span * rank)], td_group)

    def send(src, dst, send_sem, recv_sem, device):
        copy = pltpu.make_async_remote_copy(
            src_ref=src, dst_ref=dst, send_sem=send_sem, recv_sem=recv_sem,
            device_id=device, device_id_type=MESH,
        )
        copy.start()
        return copy

    low = low_lanes((64, 128))
    load_p.wait()
    load_b.wait()
    load_gc = load(6, group_coupling, gc)
    load_dc = load(7, device_coupling, dc)
    load_self = load(4, near.at[:, 0], nb_self)
    load_lc = load(5, leaf_coupling, lc)
    load_rest = load(8, near.at[:, pl.ds(1, 2)], nb_rest)
    for pair in range(leaves // 2):
        wide = []
        for leaf in (2 * pair, 2 * pair + 1):
            basis_leaf = b_own[:, leaf * ls : (leaf + 1) * ls]
            twice = jnp.concatenate([basis_leaf, basis_leaf], axis=0)
            coefs = nt(p_own[leaf], twice)
            w[leaves + leaf] = coefs.astype(BF16)
            wide.append(coefs)
        c_own[:, pair * 128 : (pair + 1) * 128] = jnp.where(low, wide[0], wide[1]).astype(BF16)

    load_t.wait()
    transfer = t_own[...]
    own_d = nt(c_own[...], jnp.concatenate([transfer, transfer], axis=0))
    own_slot = yi * cols + zi
    dbuf[own_slot] = fold_rows(own_d).astype(BF16)

    pl.semaphore_wait(barrier, (ROW - 1) + (cols - 1) + (groups - 1))

    col_copies = [
        send(dbuf.at[own_slot], dbuf.at[own_slot], col_send.at[k], col_recv.at[k], (gi, peer))
        for k, peer in enumerate(col_peers)
    ]
    to_right, to_left = jnp.where(at_end, 2, 0), jnp.where(at_start, 2, 1)
    edges = {
        "c": (halo_c, 0, c_own, c_own),
    }
    piece = half // 2
    for n, (name, buffer, from_end, from_start) in enumerate(
        (("a", halo_a, leaves - half, 0), ("b", halo_b, leaves - 2 * half, half))
    ):
        for k in (0, 1):
            edges[name + str(k)] = (
                buffer.at[:, pl.ds(k * piece, piece)],
                3 + 6 * n + 3 * k,
                p_own.at[pl.ds(from_end + k * piece, piece)],
                p_own.at[pl.ds(from_start + k * piece, piece)],
            )
    halo_copies = []

    def halo_copy(name, src, slot, k, device):
        buffer, base = edges[name][:2]
        return pltpu.make_async_remote_copy(
            src_ref=src, dst_ref=buffer.at[slot], send_sem=halo_send.at[base + k],
            recv_sem=halo_recv.at[base + slot], device_id=(gi, device), device_id_type=MESH,
        )

    has_left, has_right = li > 0, li < span - 1
    hands_on = (at_start & (zi < cols - 1)) | (at_end & (zi > 0))

    def send_halo(name):
        for k, (slot, device, needed) in enumerate(((to_right, right, has_right), (to_left, left, has_left))):
            copy = halo_copy(name, edges[name][2 + k], slot, k, device)
            pl.when(needed)(copy.start)
            halo_copies.append((needed, copy))

    def hand_on(name):
        @pl.when(hands_on)
        def _():
            buffer = edges[name][0]
            halo_copy(name, buffer.at[2], 2, 2, next_z).wait_recv()
            halo_copy(name, buffer.at[2], jnp.where(at_start, 0, 1), 2, next_z).start()

    def wait_halo(name):
        for slot, needed in ((0, has_left), (1, has_right)):
            pl.when(needed)(halo_copy(name, edges[name][0].at[2], slot, 2, next_z).wait_recv)

    def end_halo(name):
        pl.when(hands_on)(halo_copy(name, edges[name][0].at[2], 0, 2, next_z).wait_send)

    send_halo("c")
    send_halo("a0")
    send_halo("a1")

    load_td.wait()
    for j in range(cols):
        tile = pl.multiple_of((j * ROW + yi - yi % 2) * rank, 128)
        td_dup[:, j * 256 : (j + 1) * 256] = spread(td_group[:, pl.ds(tile, 128)])

    def td_of(j):
        return td_dup[:, pl.ds(pl.multiple_of(j * 256 + yi % 2 * 128, 128), 128)]

    def near_self(first, last):
        for leaf in range(first, last):
            lanes = slice(leaf * ls, (leaf + 1) * ls)
            acc[:, lanes] = nt(p_own[leaf], nb_self[leaf])

    load_self.wait()
    near_self(0, leaves)
    load_gc.wait()
    gc_dup = spread(gc[...])
    load_dc.wait()
    dc_dup = spread(dc[...])
    td_wide = jnp.concatenate([td_of(j) for j in range(cols)], axis=1)
    td_wide = jnp.concatenate([td_wide, td_wide], axis=0)

    for copy in col_copies:
        copy.wait_recv()
    col_d = jnp.concatenate([dbuf[yi * cols + j] for j in range(cols)], axis=1)
    pgbuf[yi] = fold_rows(nt(unfold_rows(col_d), td_wide))
    pg_copies = [
        send(pgbuf.at[yi], pgbuf.at[yi], row_send.at[k], row_recv.at[k], (gi, peer))
        for k, peer in enumerate(row_peers)
    ]
    send_halo("b0")
    send_halo("b1")
    mine = pl.ds(yi * cols, cols)
    d_copies = [
        send(dbuf.at[mine], dbuf.at[mine], drow_send.at[k], drow_recv.at[k], (gi, peer))
        for k, peer in enumerate(row_peers)
    ]

    for name in ("c", "a0", "a1"):
        hand_on(name)

    for copy in pg_copies:
        copy.wait_recv()
    total = pgbuf[0]
    for j in range(1, ROW):
        total = total + pgbuf[j]
    gbuf[gi] = total.astype(BF16)
    g_copies = [
        send(gbuf.at[gi], gbuf.at[gi], grp_send.at[k], grp_recv.at[k], (peer, li))
        for k, peer in enumerate(grp_peers)
    ]

    for name in ("b0", "b1"):
        hand_on(name)

    load_lc.wait()
    wait_halo("c")
    for slot, start in ((0, 0), (1, 2 * leaves)):
        for pair in range(leaves // 2):
            wide = nn(halo_c[slot, :, pair * 128 : (pair + 1) * 128], spreader()).astype(BF16)
            w[start + 2 * pair] = wide[:, :128]
            w[start + 2 * pair + 1] = wide[:, 128:]

    for pair in range(leaves // 2):
        sources = []
        matrices = []
        for leaf in (2 * pair, 2 * pair + 1):
            found = [w[clamp(leaf_list[j, leaf] - first_leaf + leaves, 3 * leaves)] for j in range(leaf_links)]
            halves = [jnp.where(low, found[j], found[j + 1]) for j in range(0, leaf_links, 2)]
            sources.append(jnp.concatenate(halves, axis=1))
            matrices.append(lc[:, leaf * leaf_links * rank : (leaf + 1) * leaf_links * rank])
        far = nt(jnp.concatenate(sources, axis=0), jnp.concatenate(matrices, axis=0))
        lf[:, pair * 128 : (pair + 1) * 128] = jnp.where(low, far[:64], far[64:])

    def leaf_of(buffer, index, count):
        return buffer[clamp(index, count)]

    def near_source(leaf, source):
        own = leaf_of(p_own, source, leaves)
        if leaf < reach:
            found = jnp.where(source >= 0, own, leaf_of(halo_a.at[0], source + half, half))
            if leaf < half:
                found = jnp.where(source < -half, leaf_of(halo_b.at[0], source + 2 * half, half), found)
        else:
            past = source - leaves
            found = jnp.where(past < 0, own, leaf_of(halo_a.at[1], past, half))
            if leaf >= leaves - half:
                found = jnp.where(past >= half, leaf_of(halo_b.at[1], past - half, half), found)
        return found

    def near_rest(leaf):
        found = [near_source(leaf, near_list[j, leaf] - first_leaf) for j in (1, 2)]
        blocks = [nb_rest[leaf, 0], nb_rest[leaf, 1]]
        return nt(jnp.concatenate(found, axis=1), jnp.concatenate(blocks, axis=1))

    load_rest.wait()
    wait_halo("a0")
    wait_halo("a1")
    for leaf in range(half, leaves - half):
        acc[:, leaf * ls : (leaf + 1) * ls] += near_rest(leaf)

    outer = list(range(half)) + list(range(leaves - half, leaves))
    handed_on = (at_start & has_left) | (at_end & has_right)

    @pl.when(jnp.logical_not(handed_on))
    def _():
        wait_halo("b0")
        wait_halo("b1")
        for leaf in outer:
            acc[:, leaf * ls : (leaf + 1) * ls] += near_rest(leaf)

    for copy in d_copies:
        copy.wait_recv()
    places = [clamp(device_list[0, j] - gi * span, span) for j in range(device_links)]
    found = [dbuf[place % ROW * cols + place // ROW] for place in places]
    d_far = nt(unfold_rows(jnp.concatenate(found, axis=1)), dc_dup)
    for copy in g_copies:
        copy.wait_recv()
    found = [gbuf[clamp(group_list[0, j], groups)] for j in range(group_links)]
    g_local = nt(unfold_rows(jnp.concatenate(found, axis=1)), gc_dup).astype(BF16)
    td_own = td_of(zi)[:, :rank]
    d_local = (d_far + nn(g_local, td_own)).astype(BF16)
    l_local = (lf[...] + nn(d_local, t_own[...])).astype(BF16)
    for pair in range(leaves // 2):
        x = l_local[:, pair * 128 : (pair + 1) * 128]
        zero = jnp.zeros_like(x)
        stacked = jnp.concatenate([jnp.where(low, x, zero), jnp.where(low, zero, x)], axis=0)
        first = slice(2 * pair * ls, (2 * pair + 1) * ls)
        second = slice((2 * pair + 1) * ls, (2 * pair + 2) * ls)
        far = nn(stacked, jnp.concatenate([b_own[:, first], b_own[:, second]], axis=0))
        for leaf, lanes, part in ((2 * pair, first, far[:64]), (2 * pair + 1, second, far[64:])):
            sums = acc[:, lanes] + part
            out[:, lanes] = sums.astype(BF16)
            if leaf in outer:
                acc[:, lanes] = sums

    @pl.when(handed_on)
    def _():
        wait_halo("b0")
        wait_halo("b1")
        for leaf in outer:
            lanes = slice(leaf * ls, (leaf + 1) * ls)
            out[:, lanes] = (acc[:, lanes] + near_rest(leaf)).astype(BF16)

    for copy in col_copies + pg_copies + d_copies + g_copies:
        copy.wait_send()
    for needed, copy in halo_copies:
        pl.when(needed)(copy.wait_send)
    for name in edges:
        end_halo(name)


def local(
    panel_values,
    cluster_basis,
    near_blocks,
    near_list,
    transfer_leaf,
    transfer_device,
    leaf_coupling,
    leaf_list,
    device_coupling,
    device_list,
    group_coupling,
    group_list,
):
    rhs, width = panel_values.shape
    leaves, near_links, ls, _ = near_blocks.shape
    rank = cluster_basis.shape[0]
    groups = lax.axis_size("group")
    span = lax.axis_size("leaf")
    cols = span // ROW
    reach = leaves // 2
    half = reach // 2
    leaf_links = leaf_list.shape[1]
    device_links = device_list.shape[1]
    group_links = group_list.shape[1]
    coefs = leaves * rank
    hbm = pl.BlockSpec(memory_space=pltpu.HBM)
    smem = pl.BlockSpec(memory_space=pltpu.SMEM)
    sizes = (groups, span, leaves, rank, ls, leaf_links, device_links, group_links, reach)
    dma = pltpu.SemaphoreType.DMA
    halo = pltpu.VMEM((3, half, rhs, ls), BF16)
    return pl.pallas_call(
        functools.partial(kernel, *sizes),
        out_shape=pltpu.VMEM((rhs, width), BF16),
        in_specs=[hbm, hbm, hbm, smem, hbm, hbm, hbm, smem, hbm, smem, hbm, smem],
        out_specs=pl.BlockSpec(memory_space=pltpu.VMEM),
        scratch_shapes=[
            pltpu.VMEM((leaves, rhs, ls), BF16),
            pltpu.VMEM((rank, width), BF16),
            pltpu.VMEM((leaves, ls, ls), BF16),
            pltpu.VMEM((leaves, near_links - 1, ls, ls), BF16),
            pltpu.VMEM((rank, coefs), BF16),
            pltpu.VMEM((rank, span * rank), BF16),
            pltpu.VMEM((rank, leaf_links * coefs), BF16),
            pltpu.VMEM((rank, device_links * rank), BF16),
            pltpu.VMEM((rank, group_links * rank), BF16),
            halo,
            halo,
            pltpu.VMEM((rhs, coefs), BF16),
            pltpu.VMEM((3, rhs, coefs), BF16),
            pltpu.VMEM((span, rhs // 2, 2 * rank), BF16),
            pltpu.VMEM((ROW, rhs // 2, 2 * rank), F32),
            pltpu.VMEM((groups, rhs // 2, 2 * rank), BF16),
            pltpu.VMEM((3 * leaves, rhs, 2 * rank), BF16),
            pltpu.VMEM((rhs, width), F32),
            pltpu.VMEM((rhs, coefs), F32),
            pltpu.VMEM((rank, cols * 4 * rank), BF16),
            dma((9,)),
            dma((15,)),
            dma((15,)),
            dma((ROW - 1,)),
            dma((ROW - 1,)),
            dma((cols - 1,)),
            dma((cols - 1,)),
            dma((ROW - 1,)),
            dma((ROW - 1,)),
            dma((groups - 1,)),
            dma((groups - 1,)),
        ],
        compiler_params=pltpu.CompilerParams(
            collective_id=0, has_side_effects=True, vmem_limit_bytes=60 * 1024 * 1024
        ),
        cost_estimate=pl.CostEstimate(flops=500_000_000, bytes_accessed=10_000_000, transcendentals=0),
    )(
        panel_values,
        cluster_basis,
        near_blocks,
        near_list.T,
        transfer_leaf,
        transfer_device,
        leaf_coupling,
        leaf_list.T,
        device_coupling,
        device_list,
        group_coupling,
        group_list,
    )


def solution(mesh):
    in_specs = (
        P(None, ("group", "leaf")),
        P(None, ("group", "leaf")),
        P(("group", "leaf"), None, None, None),
        P(("group", "leaf"), None),
        P(None, ("group", "leaf")),
        P(),
        P(None, ("group", "leaf")),
        P(("group", "leaf"), None),
        P(None, ("group", "leaf")),
        P(("group", "leaf"), None),
        P(None, "group"),
        P("group", None),
    )
    out_specs = P(None, ("group", "leaf"))
    return jax.shard_map(local, mesh=mesh, in_specs=in_specs, out_specs=out_specs, check_vma=False)
```

```python
import functools

import jax
import jax.numpy as jnp
from jax import lax
from jax.experimental import pallas as pl
from jax.experimental.pallas import tpu as pltpu
from jax.sharding import PartitionSpec as P

ROW = 4
MESH = pl.DeviceIdType.MESH
F32 = jnp.float32
BF16 = jnp.bfloat16


def nt(a, b):
    return lax.dot_general(a, b, (((1,), (1,)), ((), ())), preferred_element_type=F32)


def nn(a, b):
    return jnp.dot(a, b, preferred_element_type=F32)


def low_lanes(shape):
    return lax.broadcasted_iota(jnp.int32, shape, 1) % 128 < 64


def fold_rows(wide):
    half = wide.shape[0] // 2
    return jnp.where(low_lanes((half, 128)), wide[:half], wide[half:])


def unfold_rows(packed):
    low = low_lanes(packed.shape)
    zero = jnp.zeros_like(packed)
    return jnp.concatenate([jnp.where(low, packed, zero), jnp.where(low, zero, packed)], axis=0)


def spreader():
    row = lax.broadcasted_iota(jnp.int32, (128, 256), 0)
    col = lax.broadcasted_iota(jnp.int32, (128, 256), 1)
    return jnp.where(row == col // 128 * 64 + col % 64, 1.0, 0.0).astype(BF16)


def spread(x):
    pieces = [x[:, i : i + 128] for i in range(0, x.shape[1], 128)]
    wide = [nn(piece, spreader()).astype(BF16) for piece in pieces]
    return jnp.concatenate(wide, axis=1)


def farthest_first(count):
    return sorted(range(1, count), key=lambda k: -min(k, count - k))


def clamp(index, count):
    return jnp.minimum(jnp.maximum(index, 0), count - 1)


def kernel(
    groups, span, leaves, rank, ls, leaf_links, device_links, group_links, reach,
    panel, basis, near, near_hbm, transfer_leaf, transfer_device, leaf_coupling, leaf_hbm,
    device_coupling, device_hbm, group_coupling, group_hbm,
    out,
    p_own, b_own, nb_self, nb_rest, t_own, td_group, lc, dc, gc,
    halo_a, halo_b, c_own, halo_c, dbuf, pgbuf, gbuf,
    w, acc, lf, td_dup,
    near_list, leaf_list, device_list, group_list,
    load_sem, halo_send, halo_recv, row_send, row_recv, col_send, col_recv, drow_send, drow_recv,
    grp_send, grp_recv,
):
    gi = lax.axis_index("group")
    li = lax.axis_index("leaf")
    zi = li // ROW
    yi = li % ROW
    cols = span // ROW
    first_leaf = (gi * span + li) * leaves
    half = reach // 2
    left = zi * ROW + lax.rem(yi + ROW - 1, ROW)
    right = zi * ROW + lax.rem(yi + 1, ROW)
    at_start, at_end = yi == 0, yi == ROW - 1
    next_z = jnp.where(at_start, lax.rem(zi + 1, cols), lax.rem(zi + cols - 1, cols)) * ROW + yi

    row_peers = [zi * ROW + lax.rem(yi + k, ROW) for k in farthest_first(ROW)]
    col_peers = [lax.rem(zi + k, cols) * ROW + yi for k in farthest_first(cols)]
    grp_peers = [lax.rem(gi + k, groups) for k in farthest_first(groups)]

    barrier = pltpu.get_barrier_semaphore()
    next_left, next_right = lax.rem(li + span - 1, span), lax.rem(li + 1, span)
    for peer in col_peers:
        pl.semaphore_signal(barrier, inc=1, device_id=(gi, peer), device_id_type=MESH)
    for peer in grp_peers:
        pl.semaphore_signal(barrier, inc=1, device_id=(peer, li), device_id_type=MESH)
    for peer in row_peers + [next_left, next_right]:
        pl.semaphore_signal(barrier, inc=1, device_id=(gi, peer), device_id_type=MESH)

    def load(i, src, dst):
        copy = pltpu.make_async_copy(src, dst, load_sem.at[i])
        copy.start()
        return copy

    for leaf in range(leaves):
        pltpu.make_async_copy(panel.at[:, pl.ds(leaf * ls, ls)], p_own.at[leaf], load_sem.at[0]).start()
    load_p = pltpu.make_async_copy(p_own, p_own, load_sem.at[0])
    load_b = load(1, basis, b_own)
    load_t = load(2, transfer_leaf, t_own)
    group_start = pl.multiple_of(gi * span * rank, span * rank)
    load_td = load(3, transfer_device.at[:, pl.ds(group_start, span * rank)], td_group)

    def send(src, dst, send_sem, recv_sem, device):
        copy = pltpu.make_async_remote_copy(
            src_ref=src, dst_ref=dst, send_sem=send_sem, recv_sem=recv_sem,
            device_id=device, device_id_type=MESH,
        )
        copy.start()
        return copy

    low = low_lanes((64, 128))
    load_p.wait()
    load_b.wait()
    load_lists = [
        load(9 + i, src, dst)
        for i, (src, dst) in enumerate(
            ((near_hbm, near_list), (leaf_hbm, leaf_list), (device_hbm, device_list), (group_hbm, group_list))
        )
    ]
    load_gc = load(6, group_coupling, gc)
    load_dc = load(7, device_coupling, dc)
    load_self = load(4, near.at[:, 0], nb_self)
    load_lc = load(5, leaf_coupling, lc)
    load_rest = load(8, near.at[:, pl.ds(1, 2)], nb_rest)
    for pair in range(leaves // 2):
        wide = []
        for leaf in (2 * pair, 2 * pair + 1):
            basis_leaf = b_own[:, leaf * ls : (leaf + 1) * ls]
            twice = jnp.concatenate([basis_leaf, basis_leaf], axis=0)
            coefs = nt(p_own[leaf], twice)
            w[leaves + leaf] = coefs.astype(BF16)
            wide.append(coefs)
        c_own[:, pair * 128 : (pair + 1) * 128] = jnp.where(low, wide[0], wide[1]).astype(BF16)

    load_t.wait()
    transfer = t_own[...]
    own_d = nt(c_own[...], jnp.concatenate([transfer, transfer], axis=0))
    own_slot = yi * cols + zi
    dbuf[own_slot] = fold_rows(own_d).astype(BF16)

    pl.semaphore_wait(barrier, 2 + (ROW - 1) + (cols - 1) + (groups - 1))

    col_copies = [
        send(dbuf.at[own_slot], dbuf.at[own_slot], col_send.at[k], col_recv.at[k], (gi, peer))
        for k, peer in enumerate(col_peers)
    ]
    to_right, to_left = jnp.where(at_end, 2, 0), jnp.where(at_start, 2, 1)
    edges = {
        "c": (halo_c, 0, c_own, c_own),
    }
    piece = half // 2
    for n, (name, buffer, from_end, from_start) in enumerate(
        (("a", halo_a, leaves - half, 0), ("b", halo_b, leaves - 2 * half, half))
    ):
        for k in (0, 1):
            edges[name + str(k)] = (
                buffer.at[:, pl.ds(k * piece, piece)],
                3 + 6 * n + 3 * k,
                p_own.at[pl.ds(from_end + k * piece, piece)],
                p_own.at[pl.ds(from_start + k * piece, piece)],
            )
    halo_copies = []

    def halo_copy(name, src, slot, k, device):
        buffer, base = edges[name][:2]
        return pltpu.make_async_remote_copy(
            src_ref=src, dst_ref=buffer.at[slot], send_sem=halo_send.at[base + k],
            recv_sem=halo_recv.at[base + slot], device_id=(gi, device), device_id_type=MESH,
        )

    has_left, has_right = li > 0, li < span - 1
    hands_on = (at_start & (zi < cols - 1)) | (at_end & (zi > 0))

    def send_halo(name):
        targets = ((to_right, right, has_right), (to_left, left, has_left))
        if name == "c":
            targets = ((0, next_right, has_right), (1, next_left, has_left))
        for k, (slot, device, needed) in enumerate(targets):
            copy = halo_copy(name, edges[name][2 + k], slot, k, device)
            pl.when(needed)(copy.start)
            halo_copies.append((needed, copy))

    def hand_on(name):
        @pl.when(hands_on)
        def _():
            buffer = edges[name][0]
            halo_copy(name, buffer.at[2], 2, 2, next_z).wait_recv()
            halo_copy(name, buffer.at[2], jnp.where(at_start, 0, 1), 2, next_z).start()

    def wait_halo(name):
        for slot, needed in ((0, has_left), (1, has_right)):
            pl.when(needed)(halo_copy(name, edges[name][0].at[slot], slot, 2, next_z).wait_recv)

    def end_halo(name):
        pl.when(hands_on)(halo_copy(name, edges[name][0].at[2], 0, 2, next_z).wait_send)

    send_halo("c")
    send_halo("a0")
    send_halo("a1")

    load_td.wait()
    for j in range(cols):
        tile = pl.multiple_of((j * ROW + yi - yi % 2) * rank, 128)
        td_dup[:, j * 256 : (j + 1) * 256] = spread(td_group[:, pl.ds(tile, 128)])

    def td_of(j):
        return td_dup[:, pl.ds(pl.multiple_of(j * 256 + yi % 2 * 128, 128), 128)]

    def near_self(first, last):
        for leaf in range(first, last):
            lanes = slice(leaf * ls, (leaf + 1) * ls)
            acc[:, lanes] = nt(p_own[leaf], nb_self[leaf])

    load_self.wait()
    near_self(0, leaves)
    load_gc.wait()
    gc_dup = spread(gc[...])
    load_dc.wait()
    dc_dup = spread(dc[...])
    td_wide = jnp.concatenate([td_of(j) for j in range(cols)], axis=1)
    td_wide = jnp.concatenate([td_wide, td_wide], axis=0)

    for copy in col_copies:
        copy.wait_recv()
    col_d = jnp.concatenate([dbuf[yi * cols + j] for j in range(cols)], axis=1)
    pgbuf[yi] = fold_rows(nt(unfold_rows(col_d), td_wide))
    pg_copies = [
        send(pgbuf.at[yi], pgbuf.at[yi], row_send.at[k], row_recv.at[k], (gi, peer))
        for k, peer in enumerate(row_peers)
    ]
    send_halo("b0")
    send_halo("b1")
    mine = pl.ds(yi * cols, cols)
    d_copies = [
        send(dbuf.at[mine], dbuf.at[mine], drow_send.at[k], drow_recv.at[k], (gi, peer))
        for k, peer in enumerate(row_peers)
    ]

    for name in ("a0", "a1"):
        hand_on(name)

    for copy in pg_copies:
        copy.wait_recv()
    total = pgbuf[0]
    for j in range(1, ROW):
        total = total + pgbuf[j]
    gbuf[gi] = total.astype(BF16)
    g_copies = [
        send(gbuf.at[gi], gbuf.at[gi], grp_send.at[k], grp_recv.at[k], (peer, li))
        for k, peer in enumerate(grp_peers)
    ]

    for name in ("b0", "b1"):
        hand_on(name)

    for copy in load_lists:
        copy.wait()
    load_lc.wait()
    wait_halo("c")
    for slot, start in ((0, 0), (1, 2 * leaves)):
        for pair in range(leaves // 2):
            wide = nn(halo_c[slot, :, pair * 128 : (pair + 1) * 128], spreader()).astype(BF16)
            w[start + 2 * pair] = wide[:, :128]
            w[start + 2 * pair + 1] = wide[:, 128:]

    for pair in range(leaves // 2):
        sources = []
        matrices = []
        for leaf in (2 * pair, 2 * pair + 1):
            found = [w[clamp(leaf_list[j, leaf] - first_leaf + leaves, 3 * leaves)] for j in range(leaf_links)]
            halves = [jnp.where(low, found[j], found[j + 1]) for j in range(0, leaf_links, 2)]
            sources.append(jnp.concatenate(halves, axis=1))
            matrices.append(lc[:, leaf * leaf_links * rank : (leaf + 1) * leaf_links * rank])
        far = nt(jnp.concatenate(sources, axis=0), jnp.concatenate(matrices, axis=0))
        lf[:, pair * 128 : (pair + 1) * 128] = jnp.where(low, far[:64], far[64:])

    def leaf_of(buffer, index, count):
        return buffer[clamp(index, count)]

    def near_source(leaf, source):
        own = leaf_of(p_own, source, leaves)
        if leaf < reach:
            found = jnp.where(source >= 0, own, leaf_of(halo_a.at[0], source + half, half))
            if leaf < half:
                found = jnp.where(source < -half, leaf_of(halo_b.at[0], source + 2 * half, half), found)
        else:
            past = source - leaves
            found = jnp.where(past < 0, own, leaf_of(halo_a.at[1], past, half))
            if leaf >= leaves - half:
                found = jnp.where(past >= half, leaf_of(halo_b.at[1], past - half, half), found)
        return found

    def near_rest(leaf):
        found = [near_source(leaf, near_list[j, leaf] - first_leaf) for j in (1, 2)]
        blocks = [nb_rest[leaf, 0], nb_rest[leaf, 1]]
        return nt(jnp.concatenate(found, axis=1), jnp.concatenate(blocks, axis=1))

    load_rest.wait()
    wait_halo("a0")
    wait_halo("a1")
    for leaf in range(half, leaves - half):
        acc[:, leaf * ls : (leaf + 1) * ls] += near_rest(leaf)

    outer = list(range(half)) + list(range(leaves - half, leaves))
    handed_on = (at_start & has_left) | (at_end & has_right)

    @pl.when(jnp.logical_not(handed_on))
    def _():
        wait_halo("b0")
        wait_halo("b1")
        for leaf in outer:
            acc[:, leaf * ls : (leaf + 1) * ls] += near_rest(leaf)

    for copy in d_copies:
        copy.wait_recv()
    places = [clamp(device_list[0, j] - gi * span, span) for j in range(device_links)]
    found = [dbuf[place % ROW * cols + place // ROW] for place in places]
    d_far = nt(unfold_rows(jnp.concatenate(found, axis=1)), dc_dup)
    for copy in g_copies:
        copy.wait_recv()
    found = [gbuf[clamp(group_list[0, j], groups)] for j in range(group_links)]
    g_local = nt(unfold_rows(jnp.concatenate(found, axis=1)), gc_dup).astype(BF16)
    td_own = td_of(zi)[:, :rank]
    d_local = (d_far + nn(g_local, td_own)).astype(BF16)
    l_local = (lf[...] + nn(d_local, t_own[...])).astype(BF16)
    for pair in range(leaves // 2):
        x = l_local[:, pair * 128 : (pair + 1) * 128]
        zero = jnp.zeros_like(x)
        stacked = jnp.concatenate([jnp.where(low, x, zero), jnp.where(low, zero, x)], axis=0)
        first = slice(2 * pair * ls, (2 * pair + 1) * ls)
        second = slice((2 * pair + 1) * ls, (2 * pair + 2) * ls)
        far = nn(stacked, jnp.concatenate([b_own[:, first], b_own[:, second]], axis=0))
        for leaf, lanes, part in ((2 * pair, first, far[:64]), (2 * pair + 1, second, far[64:])):
            sums = acc[:, lanes] + part
            out[:, lanes] = sums.astype(BF16)
            if leaf in outer:
                acc[:, lanes] = sums

    @pl.when(handed_on)
    def _():
        wait_halo("b0")
        wait_halo("b1")
        for leaf in outer:
            lanes = slice(leaf * ls, (leaf + 1) * ls)
            out[:, lanes] = (acc[:, lanes] + near_rest(leaf)).astype(BF16)

    for copy in col_copies + pg_copies + d_copies + g_copies:
        copy.wait_send()
    for needed, copy in halo_copies:
        pl.when(needed)(copy.wait_send)
    for name in ("a0", "a1", "b0", "b1"):
        end_halo(name)


def local(
    panel_values,
    cluster_basis,
    near_blocks,
    near_list,
    transfer_leaf,
    transfer_device,
    leaf_coupling,
    leaf_list,
    device_coupling,
    device_list,
    group_coupling,
    group_list,
):
    rhs, width = panel_values.shape
    leaves, near_links, ls, _ = near_blocks.shape
    rank = cluster_basis.shape[0]
    groups = lax.axis_size("group")
    span = lax.axis_size("leaf")
    cols = span // ROW
    reach = leaves // 2
    half = reach // 2
    leaf_links = leaf_list.shape[1]
    device_links = device_list.shape[1]
    group_links = group_list.shape[1]
    coefs = leaves * rank
    hbm = pl.BlockSpec(memory_space=pltpu.HBM)
    sizes = (groups, span, leaves, rank, ls, leaf_links, device_links, group_links, reach)
    dma = pltpu.SemaphoreType.DMA
    halo = pltpu.VMEM((3, half, rhs, ls), BF16)
    return pl.pallas_call(
        functools.partial(kernel, *sizes),
        out_shape=pltpu.VMEM((rhs, width), BF16),
        in_specs=[hbm] * 12,
        out_specs=pl.BlockSpec(memory_space=pltpu.VMEM),
        scratch_shapes=[
            pltpu.VMEM((leaves, rhs, ls), BF16),
            pltpu.VMEM((rank, width), BF16),
            pltpu.VMEM((leaves, ls, ls), BF16),
            pltpu.VMEM((leaves, near_links - 1, ls, ls), BF16),
            pltpu.VMEM((rank, coefs), BF16),
            pltpu.VMEM((rank, span * rank), BF16),
            pltpu.VMEM((rank, leaf_links * coefs), BF16),
            pltpu.VMEM((rank, device_links * rank), BF16),
            pltpu.VMEM((rank, group_links * rank), BF16),
            halo,
            halo,
            pltpu.VMEM((rhs, coefs), BF16),
            pltpu.VMEM((2, rhs, coefs), BF16),
            pltpu.VMEM((span, rhs // 2, 2 * rank), BF16),
            pltpu.VMEM((ROW, rhs // 2, 2 * rank), F32),
            pltpu.VMEM((groups, rhs // 2, 2 * rank), BF16),
            pltpu.VMEM((3 * leaves, rhs, 2 * rank), BF16),
            pltpu.VMEM((rhs, width), F32),
            pltpu.VMEM((rhs, coefs), F32),
            pltpu.VMEM((rank, cols * 4 * rank), BF16),
            pltpu.SMEM((near_links, leaves), jnp.int32),
            pltpu.SMEM((leaf_links, leaves), jnp.int32),
            pltpu.SMEM((1, device_links), jnp.int32),
            pltpu.SMEM((1, group_links), jnp.int32),
            dma((13,)),
            dma((15,)),
            dma((15,)),
            dma((ROW - 1,)),
            dma((ROW - 1,)),
            dma((cols - 1,)),
            dma((cols - 1,)),
            dma((ROW - 1,)),
            dma((ROW - 1,)),
            dma((groups - 1,)),
            dma((groups - 1,)),
        ],
        compiler_params=pltpu.CompilerParams(
            collective_id=0, has_side_effects=True, vmem_limit_bytes=60 * 1024 * 1024
        ),
        cost_estimate=pl.CostEstimate(flops=500_000_000, bytes_accessed=10_000_000, transcendentals=0),
    )(
        panel_values,
        cluster_basis,
        near_blocks,
        near_list.T,
        transfer_leaf,
        transfer_device,
        leaf_coupling,
        leaf_list.T,
        device_coupling,
        device_list,
        group_coupling,
        group_list,
    )


def solution(mesh):
    in_specs = (
        P(None, ("group", "leaf")),
        P(None, ("group", "leaf")),
        P(("group", "leaf"), None, None, None),
        P(("group", "leaf"), None),
        P(None, ("group", "leaf")),
        P(),
        P(None, ("group", "leaf")),
        P(("group", "leaf"), None),
        P(None, ("group", "leaf")),
        P(("group", "leaf"), None),
        P(None, "group"),
        P("group", None),
    )
    out_specs = P(None, ("group", "leaf"))
    return jax.shard_map(local, mesh=mesh, in_specs=in_specs, out_specs=out_specs, check_vma=False)
```

```python
import functools

import jax
import jax.numpy as jnp
from jax import lax
from jax.experimental import pallas as pl
from jax.experimental.pallas import tpu as pltpu
from jax.sharding import PartitionSpec as P

ROW = 4
MESH = pl.DeviceIdType.MESH
F32 = jnp.float32
BF16 = jnp.bfloat16


def nt(a, b):
    return lax.dot_general(a, b, (((1,), (1,)), ((), ())), preferred_element_type=F32)


def nn(a, b):
    return jnp.dot(a, b, preferred_element_type=F32)


def low_lanes(shape):
    return lax.broadcasted_iota(jnp.int32, shape, 1) % 128 < 64


def fold_rows(wide):
    half = wide.shape[0] // 2
    return jnp.where(low_lanes((half, 128)), wide[:half], wide[half:])


def unfold_rows(packed):
    low = low_lanes(packed.shape)
    zero = jnp.zeros_like(packed)
    return jnp.concatenate([jnp.where(low, packed, zero), jnp.where(low, zero, packed)], axis=0)


def spreader():
    row = lax.broadcasted_iota(jnp.int32, (128, 256), 0)
    col = lax.broadcasted_iota(jnp.int32, (128, 256), 1)
    return jnp.where(row == col // 128 * 64 + col % 64, 1.0, 0.0).astype(BF16)


def spread(x):
    pieces = [x[:, i : i + 128] for i in range(0, x.shape[1], 128)]
    wide = [nn(piece, spreader()).astype(BF16) for piece in pieces]
    return jnp.concatenate(wide, axis=1)


def farthest_first(count):
    return sorted(range(1, count), key=lambda k: -min(k, count - k))


def clamp(index, count):
    return jnp.minimum(jnp.maximum(index, 0), count - 1)


def kernel(
    groups, span, leaves, rank, ls, leaf_links, device_links, group_links, reach,
    panel, basis, near, near_hbm, transfer_leaf, transfer_device, leaf_coupling, leaf_hbm,
    device_coupling, device_hbm, group_coupling, group_hbm,
    out,
    p_own, b_own, nb_self, nb_rest, t_own, td_group, lc, dc, gc,
    halo_a, halo_b, c_own, halo_c, dbuf, pgbuf, gbuf,
    w, acc, lf, td_dup,
    near_list, leaf_list, device_list, group_list,
    load_sem, halo_send, halo_recv, row_send, row_recv, col_send, col_recv, drow_send, drow_recv,
    grp_send, grp_recv,
):
    gi = lax.axis_index("group")
    li = lax.axis_index("leaf")
    zi = li // ROW
    yi = li % ROW
    cols = span // ROW
    first_leaf = (gi * span + li) * leaves
    half = reach // 2
    left = zi * ROW + lax.rem(yi + ROW - 1, ROW)
    right = zi * ROW + lax.rem(yi + 1, ROW)
    at_start, at_end = yi == 0, yi == ROW - 1
    next_z = jnp.where(at_start, lax.rem(zi + 1, cols), lax.rem(zi + cols - 1, cols)) * ROW + yi

    row_peers = [zi * ROW + lax.rem(yi + k, ROW) for k in farthest_first(ROW)]
    col_peers = [lax.rem(zi + k, cols) * ROW + yi for k in farthest_first(cols)]
    grp_peers = [lax.rem(gi + k, groups) for k in farthest_first(groups)]

    barrier = pltpu.get_barrier_semaphore()
    next_left, next_right = lax.rem(li + span - 1, span), lax.rem(li + 1, span)
    for peer in col_peers:
        pl.semaphore_signal(barrier, inc=1, device_id=(gi, peer), device_id_type=MESH)
    for peer in grp_peers:
        pl.semaphore_signal(barrier, inc=1, device_id=(peer, li), device_id_type=MESH)
    for peer in row_peers + [next_left, next_right]:
        pl.semaphore_signal(barrier, inc=1, device_id=(gi, peer), device_id_type=MESH)

    def load(i, src, dst):
        copy = pltpu.make_async_copy(src, dst, load_sem.at[i])
        copy.start()
        return copy

    for leaf in range(leaves):
        pltpu.make_async_copy(panel.at[:, pl.ds(leaf * ls, ls)], p_own.at[leaf], load_sem.at[0]).start()
    load_p = pltpu.make_async_copy(p_own, p_own, load_sem.at[0])
    load_b = load(1, basis, b_own)
    load_t = load(2, transfer_leaf, t_own)
    group_start = pl.multiple_of(gi * span * rank, span * rank)
    load_td = load(3, transfer_device.at[:, pl.ds(group_start, span * rank)], td_group)

    def send(src, dst, send_sem, recv_sem, device):
        copy = pltpu.make_async_remote_copy(
            src_ref=src, dst_ref=dst, send_sem=send_sem, recv_sem=recv_sem,
            device_id=device, device_id_type=MESH,
        )
        copy.start()
        return copy

    low = low_lanes((64, 128))
    load_p.wait()
    load_b.wait()
    load_lists = [
        load(9 + i, src, dst)
        for i, (src, dst) in enumerate(
            ((near_hbm, near_list), (leaf_hbm, leaf_list), (device_hbm, device_list), (group_hbm, group_list))
        )
    ]
    load_gc = load(6, group_coupling, gc)
    load_dc = load(7, device_coupling, dc)
    load_self = load(4, near.at[:, 0], nb_self)
    load_lc = load(5, leaf_coupling, lc)
    for pair in range(leaves // 2):
        wide = []
        for leaf in (2 * pair, 2 * pair + 1):
            basis_leaf = b_own[:, leaf * ls : (leaf + 1) * ls]
            twice = jnp.concatenate([basis_leaf, basis_leaf], axis=0)
            coefs = nt(p_own[leaf], twice)
            w[leaves + leaf] = coefs.astype(BF16)
            wide.append(coefs)
        c_own[:, pair * 128 : (pair + 1) * 128] = jnp.where(low, wide[0], wide[1]).astype(BF16)

    load_t.wait()
    transfer = t_own[...]
    own_d = nt(c_own[...], jnp.concatenate([transfer, transfer], axis=0))
    own_slot = yi * cols + zi
    dbuf[own_slot] = fold_rows(own_d).astype(BF16)

    pl.semaphore_wait(barrier, 2 + (ROW - 1) + (cols - 1) + (groups - 1))

    col_copies = [
        send(dbuf.at[own_slot], dbuf.at[own_slot], col_send.at[k], col_recv.at[k], (gi, peer))
        for k, peer in enumerate(col_peers)
    ]
    to_right, to_left = jnp.where(at_end, 2, 0), jnp.where(at_start, 2, 1)
    edges = {
        "c": (halo_c, 0, c_own, c_own),
    }
    piece = half // 2
    for n, (name, buffer, from_end, from_start) in enumerate(
        (("a", halo_a, leaves - half, 0), ("b", halo_b, leaves - 2 * half, half))
    ):
        for k in (0, 1):
            edges[name + str(k)] = (
                buffer.at[:, pl.ds(k * piece, piece)],
                3 + 6 * n + 3 * k,
                p_own.at[pl.ds(from_end + k * piece, piece)],
                p_own.at[pl.ds(from_start + k * piece, piece)],
            )
    halo_copies = []

    def halo_copy(name, src, slot, k, device):
        buffer, base = edges[name][:2]
        return pltpu.make_async_remote_copy(
            src_ref=src, dst_ref=buffer.at[slot], send_sem=halo_send.at[base + k],
            recv_sem=halo_recv.at[base + slot], device_id=(gi, device), device_id_type=MESH,
        )

    has_left, has_right = li > 0, li < span - 1
    hands_on = (at_start & (zi < cols - 1)) | (at_end & (zi > 0))

    def send_halo(name):
        targets = ((to_right, right, has_right), (to_left, left, has_left))
        if name == "c":
            targets = ((0, next_right, has_right), (1, next_left, has_left))
        for k, (slot, device, needed) in enumerate(targets):
            copy = halo_copy(name, edges[name][2 + k], slot, k, device)
            pl.when(needed)(copy.start)
            halo_copies.append((needed, copy))

    def hand_on(name):
        @pl.when(hands_on)
        def _():
            buffer = edges[name][0]
            halo_copy(name, buffer.at[2], 2, 2, next_z).wait_recv()
            halo_copy(name, buffer.at[2], jnp.where(at_start, 0, 1), 2, next_z).start()

    def wait_halo(name):
        for slot, needed in ((0, has_left), (1, has_right)):
            pl.when(needed)(halo_copy(name, edges[name][0].at[slot], slot, 2, next_z).wait_recv)

    def end_halo(name):
        pl.when(hands_on)(halo_copy(name, edges[name][0].at[2], 0, 2, next_z).wait_send)

    send_halo("c")
    send_halo("a0")
    send_halo("a1")

    load_td.wait()
    for j in range(cols):
        tile = pl.multiple_of((j * ROW + yi - yi % 2) * rank, 128)
        td_dup[:, j * 256 : (j + 1) * 256] = spread(td_group[:, pl.ds(tile, 128)])

    def td_of(j):
        return td_dup[:, pl.ds(pl.multiple_of(j * 256 + yi % 2 * 128, 128), 128)]

    def near_self(first, last):
        for leaf in range(first, last):
            lanes = slice(leaf * ls, (leaf + 1) * ls)
            acc[:, lanes] = nt(p_own[leaf], nb_self[leaf])

    load_self.wait()
    near_self(0, leaves)
    load_gc.wait()
    gc_dup = spread(gc[...])
    load_dc.wait()
    dc_dup = spread(dc[...])
    td_wide = jnp.concatenate([td_of(j) for j in range(cols)], axis=1)
    td_wide = jnp.concatenate([td_wide, td_wide], axis=0)

    load_rest = load(8, near.at[:, pl.ds(1, 2)], nb_rest)

    for copy in col_copies:
        copy.wait_recv()
    col_d = jnp.concatenate([dbuf[yi * cols + j] for j in range(cols)], axis=1)
    pgbuf[yi] = fold_rows(nt(unfold_rows(col_d), td_wide)).astype(BF16)
    pg_copies = [
        send(pgbuf.at[yi], pgbuf.at[yi], row_send.at[k], row_recv.at[k], (gi, peer))
        for k, peer in enumerate(row_peers)
    ]
    send_halo("b0")
    send_halo("b1")
    mine = pl.ds(yi * cols, cols)
    d_copies = [
        send(dbuf.at[mine], dbuf.at[mine], drow_send.at[k], drow_recv.at[k], (gi, peer))
        for k, peer in enumerate(row_peers)
    ]

    for name in ("a0", "a1"):
        hand_on(name)

    for copy in pg_copies:
        copy.wait_recv()
    total = pgbuf[0].astype(F32)
    for j in range(1, ROW):
        total = total + pgbuf[j].astype(F32)
    gbuf[gi] = total.astype(BF16)
    g_copies = [
        send(gbuf.at[gi], gbuf.at[gi], grp_send.at[k], grp_recv.at[k], (peer, li))
        for k, peer in enumerate(grp_peers)
    ]

    for name in ("b0", "b1"):
        hand_on(name)

    for copy in load_lists:
        copy.wait()
    load_lc.wait()
    wait_halo("c")
    for slot, start in ((0, 0), (1, 2 * leaves)):
        for pair in range(leaves // 2):
            wide = nn(halo_c[slot, :, pair * 128 : (pair + 1) * 128], spreader()).astype(BF16)
            w[start + 2 * pair] = wide[:, :128]
            w[start + 2 * pair + 1] = wide[:, 128:]

    for pair in range(leaves // 2):
        sources = []
        matrices = []
        for leaf in (2 * pair, 2 * pair + 1):
            found = [w[clamp(leaf_list[j, leaf] - first_leaf + leaves, 3 * leaves)] for j in range(leaf_links)]
            halves = [jnp.where(low, found[j], found[j + 1]) for j in range(0, leaf_links, 2)]
            sources.append(jnp.concatenate(halves, axis=1))
            matrices.append(lc[:, leaf * leaf_links * rank : (leaf + 1) * leaf_links * rank])
        far = nt(jnp.concatenate(sources, axis=0), jnp.concatenate(matrices, axis=0))
        lf[:, pair * 128 : (pair + 1) * 128] = jnp.where(low, far[:64], far[64:])

    def leaf_of(buffer, index, count):
        return buffer[clamp(index, count)]

    def near_source(leaf, source):
        own = leaf_of(p_own, source, leaves)
        if leaf < reach:
            found = jnp.where(source >= 0, own, leaf_of(halo_a.at[0], source + half, half))
            if leaf < half:
                found = jnp.where(source < -half, leaf_of(halo_b.at[0], source + 2 * half, half), found)
        else:
            past = source - leaves
            found = jnp.where(past < 0, own, leaf_of(halo_a.at[1], past, half))
            if leaf >= leaves - half:
                found = jnp.where(past >= half, leaf_of(halo_b.at[1], past - half, half), found)
        return found

    def near_rest(leaf):
        found = [near_source(leaf, near_list[j, leaf] - first_leaf) for j in (1, 2)]
        blocks = [nb_rest[leaf, 0], nb_rest[leaf, 1]]
        return nt(jnp.concatenate(found, axis=1), jnp.concatenate(blocks, axis=1))

    load_rest.wait()
    wait_halo("a0")
    wait_halo("a1")
    for leaf in range(half, leaves - half):
        acc[:, leaf * ls : (leaf + 1) * ls] += near_rest(leaf)

    outer = list(range(half)) + list(range(leaves - half, leaves))
    handed_on = (at_start & has_left) | (at_end & has_right)

    @pl.when(jnp.logical_not(handed_on))
    def _():
        wait_halo("b0")
        wait_halo("b1")
        for leaf in outer:
            acc[:, leaf * ls : (leaf + 1) * ls] += near_rest(leaf)

    for copy in d_copies:
        copy.wait_recv()
    places = [clamp(device_list[0, j] - gi * span, span) for j in range(device_links)]
    found = [dbuf[place % ROW * cols + place // ROW] for place in places]
    d_far = nt(unfold_rows(jnp.concatenate(found, axis=1)), dc_dup)
    for copy in g_copies:
        copy.wait_recv()
    found = [gbuf[clamp(group_list[0, j], groups)] for j in range(group_links)]
    g_local = nt(unfold_rows(jnp.concatenate(found, axis=1)), gc_dup).astype(BF16)
    td_own = td_of(zi)[:, :rank]
    d_local = (d_far + nn(g_local, td_own)).astype(BF16)
    l_local = (lf[...] + nn(d_local, t_own[...])).astype(BF16)
    for pair in range(leaves // 2):
        x = l_local[:, pair * 128 : (pair + 1) * 128]
        zero = jnp.zeros_like(x)
        stacked = jnp.concatenate([jnp.where(low, x, zero), jnp.where(low, zero, x)], axis=0)
        first = slice(2 * pair * ls, (2 * pair + 1) * ls)
        second = slice((2 * pair + 1) * ls, (2 * pair + 2) * ls)
        far = nn(stacked, jnp.concatenate([b_own[:, first], b_own[:, second]], axis=0))
        for leaf, lanes, part in ((2 * pair, first, far[:64]), (2 * pair + 1, second, far[64:])):
            sums = acc[:, lanes] + part
            out[:, lanes] = sums.astype(BF16)
            if leaf in outer:
                acc[:, lanes] = sums

    @pl.when(handed_on)
    def _():
        wait_halo("b0")
        wait_halo("b1")
        for leaf in outer:
            lanes = slice(leaf * ls, (leaf + 1) * ls)
            out[:, lanes] = (acc[:, lanes] + near_rest(leaf)).astype(BF16)

    for copy in col_copies + pg_copies + d_copies + g_copies:
        copy.wait_send()
    for needed, copy in halo_copies:
        pl.when(needed)(copy.wait_send)
    for name in ("a0", "a1", "b0", "b1"):
        end_halo(name)


def local(
    panel_values,
    cluster_basis,
    near_blocks,
    near_list,
    transfer_leaf,
    transfer_device,
    leaf_coupling,
    leaf_list,
    device_coupling,
    device_list,
    group_coupling,
    group_list,
):
    rhs, width = panel_values.shape
    leaves, near_links, ls, _ = near_blocks.shape
    rank = cluster_basis.shape[0]
    groups = lax.axis_size("group")
    span = lax.axis_size("leaf")
    cols = span // ROW
    reach = leaves // 2
    half = reach // 2
    leaf_links = leaf_list.shape[1]
    device_links = device_list.shape[1]
    group_links = group_list.shape[1]
    coefs = leaves * rank
    hbm = pl.BlockSpec(memory_space=pltpu.HBM)
    sizes = (groups, span, leaves, rank, ls, leaf_links, device_links, group_links, reach)
    dma = pltpu.SemaphoreType.DMA
    halo = pltpu.VMEM((3, half, rhs, ls), BF16)
    return pl.pallas_call(
        functools.partial(kernel, *sizes),
        out_shape=pltpu.VMEM((rhs, width), BF16),
        in_specs=[hbm] * 12,
        out_specs=pl.BlockSpec(memory_space=pltpu.VMEM),
        scratch_shapes=[
            pltpu.VMEM((leaves, rhs, ls), BF16),
            pltpu.VMEM((rank, width), BF16),
            pltpu.VMEM((leaves, ls, ls), BF16),
            pltpu.VMEM((leaves, near_links - 1, ls, ls), BF16),
            pltpu.VMEM((rank, coefs), BF16),
            pltpu.VMEM((rank, span * rank), BF16),
            pltpu.VMEM((rank, leaf_links * coefs), BF16),
            pltpu.VMEM((rank, device_links * rank), BF16),
            pltpu.VMEM((rank, group_links * rank), BF16),
            halo,
            halo,
            pltpu.VMEM((rhs, coefs), BF16),
            pltpu.VMEM((2, rhs, coefs), BF16),
            pltpu.VMEM((span, rhs // 2, 2 * rank), BF16),
            pltpu.VMEM((ROW, rhs // 2, 2 * rank), BF16),
            pltpu.VMEM((groups, rhs // 2, 2 * rank), BF16),
            pltpu.VMEM((3 * leaves, rhs, 2 * rank), BF16),
            pltpu.VMEM((rhs, width), F32),
            pltpu.VMEM((rhs, coefs), F32),
            pltpu.VMEM((rank, cols * 4 * rank), BF16),
            pltpu.SMEM((near_links, leaves), jnp.int32),
            pltpu.SMEM((leaf_links, leaves), jnp.int32),
            pltpu.SMEM((1, device_links), jnp.int32),
            pltpu.SMEM((1, group_links), jnp.int32),
            dma((13,)),
            dma((15,)),
            dma((15,)),
            dma((ROW - 1,)),
            dma((ROW - 1,)),
            dma((cols - 1,)),
            dma((cols - 1,)),
            dma((ROW - 1,)),
            dma((ROW - 1,)),
            dma((groups - 1,)),
            dma((groups - 1,)),
        ],
        compiler_params=pltpu.CompilerParams(
            collective_id=0, has_side_effects=True, vmem_limit_bytes=60 * 1024 * 1024
        ),
        cost_estimate=pl.CostEstimate(flops=500_000_000, bytes_accessed=10_000_000, transcendentals=0),
    )(
        panel_values,
        cluster_basis,
        near_blocks,
        near_list.T,
        transfer_leaf,
        transfer_device,
        leaf_coupling,
        leaf_list.T,
        device_coupling,
        device_list,
        group_coupling,
        group_list,
    )


def solution(mesh):
    in_specs = (
        P(None, ("group", "leaf")),
        P(None, ("group", "leaf")),
        P(("group", "leaf"), None, None, None),
        P(("group", "leaf"), None),
        P(None, ("group", "leaf")),
        P(),
        P(None, ("group", "leaf")),
        P(("group", "leaf"), None),
        P(None, ("group", "leaf")),
        P(("group", "leaf"), None),
        P(None, "group"),
        P("group", None),
    )
    out_specs = P(None, ("group", "leaf"))
    return jax.shard_map(local, mesh=mesh, in_specs=in_specs, out_specs=out_specs, check_vma=False)
```
